32 devices in a mesh: tile: 8 (over y, x, core), agent: 4 (over z).
Axes of the slice: x: 2, y: 2, z: 4, core: 2. Of those that a mesh axis runs over, the one named last changes fastest.
Arguments:
- view_tile: bfloat16 [16, 8, 768, 1024], P('agent', 'tile'), may hold values from -0.0625 to 0.0625
- block_mask: int32 [16, 8, 6, 8], P('agent', 'tile'), may hold values 0 or 1
- sinogram: float32 [16, 32, 768], P('agent'), may hold values from -24 to 24
- bin_weight: float32 [16, 32, 768], P('agent'), may hold values from 0.2 to 0.6
- model_state: float32 [8, 32, 1024], P('tile', 'agent'), may hold values from -6 to 6
- planar_state: float32 [8, 32, 1024], P('tile', 'agent'), may hold values from -6 to 6
- sagittal_state: float32 [8, 32, 1024], P('tile', 'agent'), may hold values from -6 to 6
- planar_in: float32 [9, 16], replicated, may hold values from -3 to 3
- planar_mid: float32 [3, 9, 16, 16], replicated, may hold values from -0.75 to 0.75
- planar_out: float32 [9, 16], replicated, may hold values from -0.5 to 0.5
- sagittal_in: float32 [9, 16], replicated, may hold values from -3 to 3
- sagittal_mid: float32 [3, 9, 16, 16], replicated, may hold values from -0.75 to 0.75
- sagittal_out: float32 [9, 16], replicated, may hold values from -0.5 to 0.5
Outputs:
- model_next: float32 [8, 32, 1024], P('tile', 'agent')
- planar_next: float32 [8, 32, 1024], P('tile', 'agent')
- sagittal_next: float32 [8, 32, 1024], P('tile', 'agent')
The draws below stay inside these ranges and needn't reach their ends.
All inputs are finite; a program needn't handle non-finite values. No bound on the sum of `block_mask` on one device may be relied on, other than what follows from the above.
Results may differ from the reference program's by a relative error of at most 0.0055.
Values may be sent and summed in bfloat16 or wider, within the bound.
A program may use at most 128 MiB of HBM per device.

```python
import math
import jax
import jax.numpy as jnp
from jax import lax

BINS = 768
TILE_VOX = 1024
BLOCK = 128
PX = 8
SLICES = 32
HIDDEN_SIZE = 16
MID = 3
GRAD_STEPS = 2
TAPS = 9
TILES = 8
VIEWS = 16
NX = 64
NY = 128


def place_ends(values, stream_key, least, largest):
    longest = values.shape.index(max(values.shape))
    spots = []
    for shift in (0, 1):
        where = [jax.random.randint(jax.random.fold_in(stream_key, axis), (), 0, length) for axis, length in enumerate(values.shape)]
        where[longest] = (where[longest] + shift) % values.shape[longest]
        spots.append(tuple(where))
    return values.at[spots[0]].set(least).at[spots[1]].set(largest)


def block_scale(stream_key, shape, shards, least, high):
    level = 1.0
    for axis_at, shards_of in shards:
        draws = jax.random.uniform(jax.random.fold_in(jax.random.fold_in(stream_key, 6), axis_at), (shards_of,), jnp.float32, least / len(shards), high / len(shards))
        level = level * jnp.repeat(jnp.exp(draws), shape[axis_at] // shards_of).reshape((-1,) + (1,) * (len(shape) - 1 - axis_at))
    return level


def centred(own_key, extent, spread, bound, pieces=(), kind=jnp.bfloat16):
    drawn = jax.random.normal(own_key, extent, jnp.float32) * spread
    if len(pieces) > 0:
        drawn = block_scale(own_key, extent, pieces, -0.22, 0.18) * drawn
    return jnp.clip(drawn, min=-bound, max=bound).astype(kind)


def setup_inputs(seed: int = 0) -> dict:
    seeds = jax.random.split(jax.random.key(seed), 14)
    view_tile = centred(seeds[0], (VIEWS, TILES, BINS, TILE_VOX), (TILE_VOX * TILES) ** -0.5, 0.0625, ((0, 4), (1, 8)))
    block_mask = place_ends((jax.random.randint(seeds[1], (VIEWS, TILES, BINS // BLOCK, TILE_VOX // BLOCK), 0, 3) < 2).astype(jnp.int32), jax.random.fold_in(seeds[1], 1), 0, 1)
    sinogram = centred(seeds[2], (VIEWS, SLICES, BINS), 4.0, 24.0, ((0, 4),), jnp.float32)
    bin_weight = jnp.clip(jnp.exp(math.log(0.6) - 1.0986123 * jax.random.uniform(seeds[3], (VIEWS, SLICES, BINS), jnp.float32) ** block_scale(seeds[3], (VIEWS, SLICES, BINS), ((0, 4),), -0.2, 0.2)), 0.2, 0.6)
    model_state = centred(seeds[4], (TILES, SLICES, TILE_VOX), 1.0, 6.0, ((0, 8), (1, 4)), jnp.float32)
    planar_state = centred(seeds[5], (TILES, SLICES, TILE_VOX), 1.0, 6.0, ((0, 8), (1, 4)), jnp.float32)
    sagittal_state = centred(seeds[6], (TILES, SLICES, TILE_VOX), 1.0, 6.0, ((0, 8), (1, 4)), jnp.float32)
    planar_in = centred(seeds[7], (TAPS, HIDDEN_SIZE), (TAPS // 2) ** -0.5, 3.0, (), jnp.float32)
    planar_mid = centred(seeds[8], (MID, TAPS, HIDDEN_SIZE, HIDDEN_SIZE), (TAPS * HIDDEN_SIZE // 2) ** -0.5, 0.75, (), jnp.float32)
    planar_out = centred(seeds[9], (TAPS, HIDDEN_SIZE), (TAPS * HIDDEN_SIZE) ** -0.5, 0.5, (), jnp.float32)
    sagittal_in = centred(seeds[10], (TAPS, HIDDEN_SIZE), (TAPS // 2) ** -0.5, 3.0, (), jnp.float32)
    sagittal_mid = centred(seeds[11], (MID, TAPS, HIDDEN_SIZE, HIDDEN_SIZE), (TAPS * HIDDEN_SIZE // 2) ** -0.5, 0.75, (), jnp.float32)
    sagittal_out = centred(seeds[12], (TAPS, HIDDEN_SIZE), (TAPS * HIDDEN_SIZE) ** -0.5, 0.5, (), jnp.float32)
    return dict(view_tile=view_tile, block_mask=block_mask, sinogram=sinogram, bin_weight=bin_weight, model_state=model_state, planar_state=planar_state, sagittal_state=sagittal_state, planar_in=planar_in, planar_mid=planar_mid, planar_out=planar_out, sagittal_in=sagittal_in, sagittal_mid=sagittal_mid, sagittal_out=sagittal_out)


step_size = 0.5
prox_weight = 1.0
relax_rate = 0.5
share_model = 0.5
share_plane = 0.25
share_side = 0.25
highest = lax.Precision.HIGHEST


def blocked(matrix, pattern):
    leading = matrix.shape[:-2]
    rows_in = matrix.shape[-2]
    cols_in = matrix.shape[-1]
    row_blocks = pattern.shape[-2]
    col_blocks = pattern.shape[-1]
    tiled_grid = matrix.reshape(leading + (row_blocks, rows_in // row_blocks, col_blocks, cols_in // col_blocks))
    keeper = pattern.astype(matrix.dtype)[..., :, None, :, None]
    return (tiled_grid * keeper).reshape(matrix.shape)


def convolve(activity, kernel):
    span_rows = activity.shape[2] - 2
    span_cols = activity.shape[3] - 2
    summed = jnp.zeros((kernel.shape[1], activity.shape[1], span_rows, span_cols), jnp.float32)
    for offset in range(9):
        row_off = offset // 3
        col_off = offset % 3
        window = activity[:, :, row_off:row_off + span_rows, col_off:col_off + span_cols]
        summed = summed + jnp.einsum("oc,cbhw->obhw", kernel[offset], window, precision=highest)
    return summed


def pad_both(activity):
    return jnp.pad(activity, ((0, 0), (0, 0), (1, 1), (1, 1)))


def kernels(first_in, middle, last_out):
    return [first_in[:, :, None]] + [middle[member] for member in range(middle.shape[0])] + [last_out[:, None, :]]


def denoise(volume, first_in, middle, last_out):
    kernel_list = kernels(first_in, middle, last_out)
    current = volume[None]
    for position, kernel in enumerate(kernel_list):
        current = convolve(pad_both(current), kernel)
        if position + 1 < len(kernel_list):
            current = jax.nn.relu(current)
    return volume - current[0]


def to_volume(state):
    return state.reshape(TILES, SLICES, PX, NY).transpose(1, 0, 2, 3).reshape(SLICES, NX, NY)


def from_volume(volume):
    return volume.reshape(SLICES, TILES, PX, NY).transpose(1, 0, 2, 3).reshape(TILES, SLICES, PX * NY)


def reference(view_tile, block_mask, sinogram, bin_weight, model_state, planar_state, sagittal_state, planar_in, planar_mid, planar_out, sagittal_in, sagittal_mid, sagittal_out):
    guess = model_state
    for iteration in range(GRAD_STEPS):
        guess_low = lax.optimization_barrier(guess.astype(jnp.bfloat16)).astype(jnp.float32)

        def forward(operands):
            matrix, pattern = operands
            masked = blocked(matrix, pattern).astype(jnp.float32)
            return jnp.einsum("tsk,tbk->sb", guess_low, masked, precision=highest)

        projection = lax.map(forward, (view_tile, block_mask))
        misfit = lax.optimization_barrier((bin_weight * (projection - sinogram)).astype(jnp.bfloat16)).astype(jnp.float32)

        def backward(running, triple):
            matrix, pattern, residue = triple
            masked = blocked(matrix, pattern).astype(jnp.float32)
            return running + jnp.einsum("sb,tbk->tsk", residue, masked, precision=highest), None

        gradient, leftover = lax.scan(backward, jnp.zeros(guess.shape, jnp.float32), (view_tile, block_mask, misfit))
        guess = guess - step_size * (gradient + prox_weight * (guess - model_state))
    model_image = guess
    planar_image = from_volume(denoise(to_volume(planar_state), planar_in, planar_mid, planar_out))
    side_volume = to_volume(sagittal_state).transpose(1, 0, 2)
    sagittal_image = from_volume(denoise(side_volume, sagittal_in, sagittal_mid, sagittal_out).transpose(1, 0, 2))
    reflect_model = 2.0 * model_image - model_state
    reflect_plane = 2.0 * planar_image - planar_state
    reflect_side = 2.0 * sagittal_image - sagittal_state
    consensus = share_model * reflect_model + share_plane * reflect_plane + share_side * reflect_side
    model_next = (1.0 - relax_rate) * model_state + relax_rate * (2.0 * consensus - reflect_model)
    planar_next = (1.0 - relax_rate) * planar_state + relax_rate * (2.0 * consensus - reflect_plane)
    sagittal_next = (1.0 - relax_rate) * sagittal_state + relax_rate * (2.0 * consensus - reflect_side)
    return (model_next, planar_next, sagittal_next)
```

```python
import functools

import jax
import jax.numpy as jnp
from jax import lax
from jax.experimental import pallas as pl
from jax.experimental.pallas import tpu as pltpu
from jax.sharding import PartitionSpec as P

PX = 8
GRAD_STEPS = 2


step_size = 0.5
prox_weight = 1.0
relax_rate = 0.5
share_model = 0.5
share_plane = 0.25
share_side = 0.25
highest = lax.Precision.HIGHEST


def with_halo(block, sides, width):
    for axis, dim in sides:
        count = lax.axis_size(axis)
        forward = [(i, i + 1) for i in range(count - 1)]
        backward = [(target, source) for source, target in forward]
        low = lax.ppermute(
            lax.slice_in_dim(block, block.shape[dim] - width, None, axis=dim), axis, forward
        )
        high = lax.ppermute(lax.slice_in_dim(block, 0, width, axis=dim), axis, backward)
        block = jnp.concatenate([low, block, high], axis=dim)
    return block


def blocked(matrix, pattern):
    leading = matrix.shape[:-2]
    rows_in = matrix.shape[-2]
    cols_in = matrix.shape[-1]
    row_blocks = pattern.shape[-2]
    col_blocks = pattern.shape[-1]
    tiled_grid = matrix.reshape(
        leading + (row_blocks, rows_in // row_blocks, col_blocks, cols_in // col_blocks)
    )
    keeper = pattern.astype(matrix.dtype)[..., :, None, :, None]
    return (tiled_grid * keeper).reshape(matrix.shape)


def convolve(activity, kernel):
    span_rows = activity.shape[2] - 2
    span_cols = activity.shape[3] - 2
    summed = jnp.zeros((kernel.shape[1], activity.shape[1], span_rows, span_cols), jnp.float32)
    for offset in range(9):
        row_off = offset // 3
        col_off = offset % 3
        window = activity[:, :, row_off : row_off + span_rows, col_off : col_off + span_cols]
        summed = summed + jnp.einsum("oc,cbhw->obhw", kernel[offset], window, precision=highest)
    return summed


def pad_both(activity):
    return jnp.pad(activity, ((0, 0), (0, 0), (1, 1), (1, 1)))


def pad_cols(activity):
    return jnp.pad(activity, ((0, 0), (0, 0), (0, 0), (1, 1)))


def kernels(first_in, middle, last_out):
    return (
        [first_in[:, :, None]]
        + [middle[member] for member in range(middle.shape[0])]
        + [last_out[:, None, :]]
    )


def denoise(volume, first_in, middle, last_out):
    kernel_list = kernels(first_in, middle, last_out)
    current = volume[None]
    for position, kernel in enumerate(kernel_list):
        current = convolve(pad_both(current), kernel)
        if position + 1 < len(kernel_list):
            current = jax.nn.relu(current)
    return volume - current[0]


def margin(activity, reach):
    return with_halo(activity, (("tile", 2),), reach)


def planar_pass(volume, kernel_list):
    layers_all = len(kernel_list)
    current = volume[None]
    for position, kernel in enumerate(kernel_list):
        current = convolve(pad_cols(margin(current, 1)), kernel)
        if position + 1 < layers_all:
            current = jax.nn.relu(current)
    return volume - current[0]


def plain_device(
    view_tile,
    block_mask,
    sinogram,
    bin_weight,
    model_state,
    planar_state,
    sagittal_state,
    planar_in,
    planar_mid,
    planar_out,
    sagittal_in,
    sagittal_mid,
    sagittal_out,
):
    slices_own = model_state.shape[1]
    voxels = model_state.shape[2]
    views_here = view_tile.shape[0]
    bins_all = view_tile.shape[2]
    masked = blocked(view_tile[:, 0], block_mask[:, 0])
    slices_all = slices_own * lax.axis_size("agent")
    rows_all = views_here * slices_all
    sino_rows = sinogram.reshape(rows_all, bins_all)
    weight_rows = bin_weight.reshape(rows_all, bins_all)
    own_anchor = model_state[0]
    guess_own = own_anchor
    guess_low = lax.all_gather(own_anchor.astype(jnp.bfloat16), "agent", axis=0, tiled=True)
    for iteration in range(GRAD_STEPS):
        partial_value = jnp.einsum(
            "sk,vbk->vsb", guess_low, masked, preferred_element_type=jnp.float32
        ).reshape(rows_all, bins_all)
        summed = lax.psum(partial_value, "tile")
        misfit = (weight_rows * (summed - sino_rows)).astype(jnp.bfloat16)
        misfit = misfit.reshape(views_here, slices_all, bins_all)
        grad_own = lax.psum_scatter(
            jnp.einsum("vsb,vbk->sk", misfit, masked, preferred_element_type=jnp.float32).astype(
                jnp.bfloat16
            ),
            "agent",
            scatter_dimension=0,
            tiled=True,
        ).astype(jnp.float32)
        guess_own = guess_own - step_size * (grad_own + prox_weight * (guess_own - own_anchor))
        if iteration + 1 < GRAD_STEPS:
            guess_low = lax.all_gather(guess_own.astype(jnp.bfloat16), "agent", axis=0, tiled=True)
    model_image = guess_own[None]
    plane_volume = planar_state[0].reshape(slices_own, PX, voxels // PX)
    plane_clean = planar_pass(plane_volume, kernels(planar_in, planar_mid, planar_out))
    planar_image = plane_clean.reshape(1, slices_own, voxels)
    side_volume = sagittal_state[0].reshape(slices_own, PX, voxels // PX)
    regrouped = lax.all_to_all(side_volume, "agent", split_axis=1, concat_axis=0, tiled=True)
    side_clean = denoise(
        regrouped.transpose(1, 0, 2), sagittal_in, sagittal_mid, sagittal_out
    ).transpose(1, 0, 2)
    returned = lax.all_to_all(side_clean, "agent", split_axis=0, concat_axis=1, tiled=True)
    sagittal_image = returned.reshape(1, slices_own, voxels)
    reflect_model = 2.0 * model_image - model_state
    reflect_plane = 2.0 * planar_image - planar_state
    reflect_side = 2.0 * sagittal_image - sagittal_state
    consensus = (
        share_model * reflect_model + share_plane * reflect_plane + share_side * reflect_side
    )
    model_next = (1.0 - relax_rate) * model_state + relax_rate * (2.0 * consensus - reflect_model)
    planar_next = (1.0 - relax_rate) * planar_state + relax_rate * (2.0 * consensus - reflect_plane)
    sagittal_next = (1.0 - relax_rate) * sagittal_state + relax_rate * (
        2.0 * consensus - reflect_side
    )
    return (model_next, planar_next, sagittal_next)


LANES = 128
FRAME = 16
HIGH_ROWS = 24
MESH = pl.DeviceIdType.MESH


def split_low(x):
    high = x.astype(jnp.bfloat16)
    low = (x - high.astype(jnp.float32)).astype(jnp.bfloat16)
    return high, low


def dot(a, b):
    return jnp.dot(a, b, preferred_element_type=jnp.float32)


def exact_dot(a, b):
    return jnp.dot(a, b, precision=highest, preferred_element_type=jnp.float32)


def iota(shape, dim):
    return lax.broadcasted_iota(jnp.int32, shape, dim)


def pack(x):
    half = x.shape[1] // 2
    return jnp.concatenate([x[:, :half], x[:, half:]], axis=0).astype(jnp.bfloat16)


def unpack(x):
    x = x.astype(jnp.float32)
    rows = x.shape[0] // 2
    return jnp.concatenate([x[:rows], x[rows:]], axis=1)


def column_shifts(h):
    lane = iota((h.shape[0], LANES), 1)
    befores, afters = [], []
    for start in range(0, h.shape[1], LANES):
        part = h[:, start : start + LANES]
        befores.append(jnp.where(lane == 0, 0.0, pltpu.roll(part, 1, axis=1)))
        afters.append(jnp.where(lane == LANES - 1, 0.0, pltpu.roll(part, LANES - 1, axis=1)))
    return jnp.concatenate(
        [jnp.concatenate(befores, axis=1), h, jnp.concatenate(afters, axis=1)], axis=0
    )


def build_weights(d, in_ref, mid_ref, out_ref, w_first, w_mid, w_last):
    layers, taps, hidden, _ = mid_ref.shape
    wide = FRAME * hidden
    spread = (iota((hidden, wide), 1) % hidden == iota((hidden, wide), 0)).astype(jnp.float32)
    gather = (iota((wide, hidden), 0) % hidden == iota((wide, hidden), 1)).astype(jnp.float32)
    columns = lax.dot_general(
        gather, in_ref[...], (((1,), (1,)), ((), ())), precision=highest,
        preferred_element_type=jnp.float32,
    )
    high, low = split_low(columns)
    high, low = high.astype(jnp.float32), low.astype(jnp.float32)
    depth = w_first.shape[2]
    offset = iota((wide, depth), 1) - iota((wide, depth), 0) // hidden
    first = jnp.zeros((wide, depth), jnp.float32)
    for turn, source in enumerate((high, high, low)):
        for tap in range(taps):
            a, e = tap // 3, tap % 3
            place = 3 * HIGH_ROWS * turn + HIGH_ROWS * e + a
            first = jnp.where(offset == place, source[:, tap : tap + 1], first)
    w_first[d] = first.astype(jnp.bfloat16)
    band = iota((wide, wide), 1) // hidden - iota((wide, wide), 0) // hidden
    for layer in range(layers):
        for e in range(3):
            value = jnp.zeros((wide, wide), jnp.float32)
            for a in range(3):
                tile = exact_dot(mid_ref[layer, 3 * a + e], spread)
                value = jnp.where(band == a - 1, jnp.concatenate([tile] * FRAME, axis=0), value)
            high, low = split_low(value)
            w_mid[d * layers + layer, 0, :, e * wide : (e + 1) * wide] = high
            w_mid[d * layers + layer, 1, :, e * wide : (e + 1) * wide] = low
    rows = exact_dot(out_ref[...], spread)
    margin_rows = layers
    shift = iota((PX, wide), 1) // hidden - iota((PX, wide), 0)
    for e in range(3):
        value = jnp.zeros((PX, wide), jnp.float32)
        for a in range(3):
            tap = 3 * a + e
            row = jnp.broadcast_to(rows[tap : tap + 1], (PX, wide))
            value = jnp.where(shift == margin_rows + a, row, value)
        high, low = split_low(value)
        both = jnp.concatenate([high.astype(jnp.float32), low.astype(jnp.float32)], axis=0)
        w_last[d, :, e * wide : (e + 1) * wide] = both.astype(jnp.bfloat16)


def denoise_unit(d, at, width, layers, hidden, place, count, field, w_first, w_mid, w_last, clean):
    lanes = slice(at, at + width)
    wide = FRAME * hidden
    frame_row = iota((wide, width), 0) // hidden
    above = (layers + 1) - place * PX
    below = (layers + 1) + (count - place) * PX
    inside = (frame_row >= above) & (frame_row < below)

    def active(x):
        return jnp.where(inside, jnp.maximum(x, 0.0), 0.0)

    shifted = column_shifts(field[d, :, lanes])
    high = shifted.astype(jnp.bfloat16).astype(jnp.float32)
    spare = w_first.shape[2] - 3 * shifted.shape[0]
    stacked = jnp.concatenate(
        [high, shifted - high, high, jnp.zeros((spare, width), jnp.float32)], axis=0
    ).astype(jnp.bfloat16)
    h = active(dot(w_first[d], stacked))

    def layer_step(layer, h):
        high, low = split_low(column_shifts(h))
        w_high, w_low = w_mid[d * layers + layer, 0], w_mid[d * layers + layer, 1]
        return active(dot(w_high, high) + dot(w_high, low) + dot(w_low, high))

    h = lax.fori_loop(0, layers, layer_step, h)
    high, low = split_low(column_shifts(h))
    first = dot(w_last[d], high)
    second = dot(w_last[d], low)
    change = first[:PX] + first[PX : 2 * PX] + second[:PX]
    own = field[d, layers + 2 : layers + 2 + PX, lanes]
    clean[d, :, lanes] = own - change


def kernel(
    tiles, agents,
    view_hbm, mask_ref, sino_hbm, weight_hbm, model_ref, planar_ref, sagittal_ref,
    pin_ref, pmid_ref, pout_ref, sin_ref, smid_ref, sout_ref,
    model_out, planar_out, sagittal_out,
    masked, sino, weight, guess_all, part_send, part_recv, mis_all, grad_send, grad_recv,
    own_plane, halo, field, w_first, w_mid, w_last, clean,
    local_sem, send_agent, recv_agent, send_tile, recv_tile, send_halo, recv_halo,
):
    tile, agent = lax.axis_index("tile"), lax.axis_index("agent")
    views, bins = masked.shape[0], masked.shape[1]
    own_slices, voxels = model_ref.shape[1], model_ref.shape[2]
    layers, _, hidden, _ = pmid_ref.shape
    cells = voxels // PX
    slices_all = own_slices * agents

    load_view = pltpu.make_async_copy(view_hbm.at[:, 0], masked, local_sem.at[0])
    load_sino = pltpu.make_async_copy(sino_hbm.at[tile], sino, local_sem.at[1])
    load_weight = pltpu.make_async_copy(weight_hbm.at[tile], weight, local_sem.at[2])
    load_view.start()
    load_sino.start()
    load_weight.start()

    barrier = pltpu.get_barrier_semaphore()
    for k in range(1, agents):
        pl.semaphore_signal(
            barrier, inc=1, device_id=(tile, lax.rem(agent + k, agents)), device_id_type=MESH
        )
    for k in range(1, tiles):
        pl.semaphore_signal(
            barrier, inc=1, device_id=(lax.rem(tile + k, tiles), agent), device_id_type=MESH
        )
    anchor = model_ref[0]
    guess_all[0, agent] = pack(anchor)
    for row in range(PX):
        for piece in range(own_slices):
            own_plane[row : row + 1, piece * cells : (piece + 1) * cells] = planar_ref[
                0, piece : piece + 1, row * cells : (row + 1) * cells
            ]
    pl.semaphore_wait(barrier, agents + tiles - 2)

    sent = []

    def to_agent(src, dst, step, phase, k):
        copy = pltpu.make_async_remote_copy(
            src_ref=src, dst_ref=dst, send_sem=send_agent.at[step, phase, k],
            recv_sem=recv_agent.at[step, phase, k],
            device_id=(tile, lax.rem(agent + k, agents)), device_id_type=MESH,
        )
        copy.start()
        sent.append(copy)
        return copy

    def to_tile(src, dst, step, phase, k):
        copy = pltpu.make_async_remote_copy(
            src_ref=src, dst_ref=dst, send_sem=send_tile.at[step, phase, k],
            recv_sem=recv_tile.at[step, phase, k],
            device_id=(lax.rem(tile + k, tiles), agent), device_id_type=MESH,
        )
        copy.start()
        sent.append(copy)
        return copy

    def share_guess(step):
        return [
            to_agent(guess_all.at[step, agent], guess_all.at[step, agent], step, 0, k)
            for k in range(1, agents)
        ]

    waiting = share_guess(0)
    halos = []
    sides = (
        (own_plane, (lax.rem(tile + 1, tiles), agent)),
        (own_plane, (lax.rem(tile + tiles - 1, tiles), agent)),
        (sagittal_ref.at[0], (tile, lax.rem(agent + 1, agents))),
        (sagittal_ref.at[0], (tile, lax.rem(agent + agents - 1, agents))),
    )
    for k, (source, target) in enumerate(sides):
        copy = pltpu.make_async_remote_copy(
            src_ref=source, dst_ref=halo.at[k], send_sem=send_halo.at[k],
            recv_sem=recv_halo.at[k], device_id=target, device_id_type=MESH,
        )
        copy.start()
        halos.append(copy)
        sent.append(copy)

    build_weights(0, pin_ref, pmid_ref, pout_ref, w_first, w_mid, w_last)
    build_weights(1, sin_ref, smid_ref, sout_ref, w_first, w_mid, w_last)

    load_view.wait()
    row_blocks, col_blocks = mask_ref.shape[2], mask_ref.shape[3]
    block_rows, block_cols = bins // row_blocks, voxels // col_blocks
    widen = (
        iota((col_blocks, voxels), 1) // block_cols == iota((col_blocks, voxels), 0)
    ).astype(jnp.float32)
    for view in range(views):
        keep = exact_dot(mask_ref[view, 0].astype(jnp.float32), widen)
        for block in range(row_blocks):
            at = slice(block * block_rows, (block + 1) * block_rows)
            row = jnp.broadcast_to(keep[block : block + 1], (block_rows, voxels))
            masked[view, at] = masked[view, at] * row.astype(jnp.bfloat16)

    width = 2 * cells
    work = [(d, at) for d in range(2) for at in range(0, PX * cells, width)]
    places = ((tile, tiles), (agent, agents))

    def some_work():
        if work:
            d, at = work.pop(0)
            denoise_unit(
                d, at, width, layers, hidden, places[d][0], places[d][1],
                field, w_first, w_mid, w_last, clean,
            )

    def fill_fields():
        reach = layers + 2
        for copy in halos:
            copy.wait_recv()
        for d, own in ((0, own_plane[...]), (1, sagittal_ref[0])):
            place, count = places[d]
            low = halo[2 * d, PX - reach : PX]
            high = halo[2 * d + 1, 0:reach]
            field[d, 0:reach] = jnp.where(place > 0, low, jnp.zeros_like(low))
            field[d, reach : reach + PX] = own
            field[d, reach + PX : 2 * reach + PX] = jnp.where(
                place < count - 1, high, jnp.zeros_like(high)
            )
            rest = HIGH_ROWS - 2 * reach - PX
            field[d, 2 * reach + PX : HIGH_ROWS] = jnp.zeros((rest, PX * cells), jnp.float32)

    guess = anchor
    chunk = sino.shape[0]
    per_view = slices_all // chunk
    for step in range(GRAD_STEPS):
        for copy in waiting:
            copy.wait_recv()
        guess_low = jnp.concatenate(
            [unpack(guess_all[step, a]) for a in range(agents)], axis=0
        ).astype(jnp.bfloat16)
        for view in range(views):
            partial = lax.dot_general(
                guess_low, masked[view], (((1,), (1,)), ((), ())),
                preferred_element_type=jnp.float32,
            ).astype(jnp.bfloat16)
            for piece in range(per_view):
                part_send[step, view * per_view + piece] = partial[
                    piece * chunk : (piece + 1) * chunk
                ]
        waiting = [
            to_tile(
                part_send.at[step, lax.rem(tile + k, tiles)], part_recv.at[step, k], step, 0, k
            )
            for k in range(1, tiles)
        ]
        if step == 0:
            fill_fields()
            load_sino.wait()
            load_weight.wait()
        some_work()
        total = part_send[step, tile].astype(jnp.float32)
        for k, copy in enumerate(waiting):
            copy.wait_recv()
            total = total + part_recv[step, k + 1].astype(jnp.float32)
        mis_all[step, tile] = (weight[...] * (total - sino[...])).astype(jnp.bfloat16)
        waiting = [
            to_tile(mis_all.at[step, tile], mis_all.at[step, tile], step, 1, k)
            for k in range(1, tiles)
        ]
        some_work()
        for copy in waiting:
            copy.wait_recv()
        gradient = jnp.zeros((slices_all, voxels), jnp.float32)
        for view in range(views):
            misfit = jnp.concatenate(
                [mis_all[step, view * per_view + piece] for piece in range(per_view)], axis=0
            )
            gradient = gradient + dot(misfit, masked[view])
        for a in range(agents):
            grad_send[step, a] = pack(gradient[a * own_slices : (a + 1) * own_slices])
        waiting = [
            to_agent(
                grad_send.at[step, lax.rem(agent + k, agents)], grad_recv.at[step, k], step, 1, k
            )
            for k in range(1, agents)
        ]
        some_work()
        total = unpack(grad_send[step, agent])
        for k, copy in enumerate(waiting):
            copy.wait_recv()
            total = total + unpack(grad_recv[step, k + 1])
        guess = guess - step_size * (total + prox_weight * (guess - anchor))
        if step + 1 < GRAD_STEPS:
            guess_all[step + 1, agent] = pack(guess)
            waiting = share_guess(step + 1)
            some_work()
    while work:
        some_work()

    for row in range(PX):
        for piece in range(own_slices):
            planar_out[0, piece : piece + 1, row * cells : (row + 1) * cells] = clean[
                0, row : row + 1, piece * cells : (piece + 1) * cells
            ]
    planar_image = planar_out[0]
    sagittal_image = clean[1]
    planar_own, sagittal_own = planar_ref[0], sagittal_ref[0]
    reflect_model = 2.0 * guess - anchor
    reflect_plane = 2.0 * planar_image - planar_own
    reflect_side = 2.0 * sagittal_image - sagittal_own
    consensus = (
        share_model * reflect_model + share_plane * reflect_plane + share_side * reflect_side
    )
    keep_rate = 1.0 - relax_rate
    model_out[0] = keep_rate * anchor + relax_rate * (2.0 * consensus - reflect_model)
    planar_out[0] = keep_rate * planar_own + relax_rate * (2.0 * consensus - reflect_plane)
    sagittal_out[0] = keep_rate * sagittal_own + relax_rate * (2.0 * consensus - reflect_side)
    for copy in sent:
        copy.wait_send()


def per_device(*arguments):
    (view_tile, block_mask, sinogram, bin_weight, model_state, planar_state, sagittal_state,
     planar_in, planar_mid, planar_out, sagittal_in, sagittal_mid, sagittal_out) = arguments
    tiles, agents = lax.axis_size("tile"), lax.axis_size("agent")
    views, _, bins, voxels = view_tile.shape
    own_slices = model_state.shape[1]
    layers, taps, hidden, _ = planar_mid.shape
    rows_all = views * own_slices * agents
    chunk = rows_all // tiles
    fits = (
        chunk * tiles == rows_all
        and chunk % 16 == 0
        and (own_slices * agents) % chunk == 0
        and own_slices == PX
        and voxels == PX * LANES
        and PX + 2 * (layers + 1) <= FRAME
        and min(tiles, agents) > 1
    )
    if not fits:
        return plain_device(*arguments)
    bf16, f32 = jnp.bfloat16, jnp.float32
    vmem = pl.BlockSpec(memory_space=pltpu.VMEM)
    anywhere = pl.BlockSpec(memory_space=pl.ANY)
    wide = FRAME * hidden
    plane = (2 * own_slices, voxels // 2)
    depth = (9 * HIGH_ROWS + 15) // 16 * 16
    dma = pltpu.SemaphoreType.DMA
    return pl.pallas_call(
        functools.partial(kernel, tiles, agents),
        out_shape=[jax.ShapeDtypeStruct(model_state.shape, f32)] * 3,
        in_specs=[anywhere, vmem, anywhere, anywhere] + [vmem] * 9,
        out_specs=[vmem] * 3,
        scratch_shapes=[
            pltpu.VMEM((views, bins, voxels), bf16),
            pltpu.VMEM((chunk, bins), f32),
            pltpu.VMEM((chunk, bins), f32),
            pltpu.VMEM((GRAD_STEPS, agents) + plane, bf16),
            pltpu.VMEM((GRAD_STEPS, tiles, chunk, bins), bf16),
            pltpu.VMEM((GRAD_STEPS, tiles, chunk, bins), bf16),
            pltpu.VMEM((GRAD_STEPS, tiles, chunk, bins), bf16),
            pltpu.VMEM((GRAD_STEPS, agents) + plane, bf16),
            pltpu.VMEM((GRAD_STEPS, agents) + plane, bf16),
            pltpu.VMEM((PX, own_slices * (voxels // PX)), f32),
            pltpu.VMEM((4, PX, voxels), f32),
            pltpu.VMEM((2, HIGH_ROWS, voxels), f32),
            pltpu.VMEM((2, wide, depth), bf16),
            pltpu.VMEM((2 * layers, 2, wide, 3 * wide), bf16),
            pltpu.VMEM((2, 2 * PX, 3 * wide), bf16),
            pltpu.VMEM((2, PX, voxels), f32),
            dma((3,)),
            dma((GRAD_STEPS, 2, agents)),
            dma((GRAD_STEPS, 2, agents)),
            dma((GRAD_STEPS, 2, tiles)),
            dma((GRAD_STEPS, 2, tiles)),
            dma((4,)),
            dma((4,)),
        ],
        compiler_params=pltpu.CompilerParams(
            collective_id=0, has_side_effects=True, vmem_limit_bytes=48 * 1024 * 1024
        ),
    )(
        view_tile,
        block_mask,
        sinogram.reshape(tiles, chunk, bins),
        bin_weight.reshape(tiles, chunk, bins),
        model_state, planar_state, sagittal_state,
        planar_in, planar_mid, planar_out, sagittal_in, sagittal_mid, sagittal_out,
    )


def solution(mesh):
    return jax.shard_map(
        per_device,
        mesh=mesh,
        in_specs=(
            P("agent", "tile", None, None),
            P("agent", "tile", None, None),
            P("agent", None, None),
            P("agent", None, None),
            P("tile", "agent", None),
            P("tile", "agent", None),
            P("tile", "agent", None),
            P(),
            P(),
            P(),
            P(),
            P(),
            P(),
        ),
        out_specs=(P("tile", "agent", None), P("tile", "agent", None), P("tile", "agent", None)),
        check_vma=False,
    )
```

```python
import functools

import jax
import jax.numpy as jnp
from jax import lax
from jax.experimental import pallas as pl
from jax.experimental.pallas import tpu as pltpu
from jax.sharding import PartitionSpec as P

PX = 8
GRAD_STEPS = 2


step_size = 0.5
prox_weight = 1.0
relax_rate = 0.5
share_model = 0.5
share_plane = 0.25
share_side = 0.25
highest = lax.Precision.HIGHEST


def with_halo(block, sides, width):
    for axis, dim in sides:
        count = lax.axis_size(axis)
        forward = [(i, i + 1) for i in range(count - 1)]
        backward = [(target, source) for source, target in forward]
        low = lax.ppermute(
            lax.slice_in_dim(block, block.shape[dim] - width, None, axis=dim), axis, forward
        )
        high = lax.ppermute(lax.slice_in_dim(block, 0, width, axis=dim), axis, backward)
        block = jnp.concatenate([low, block, high], axis=dim)
    return block


def blocked(matrix, pattern):
    leading = matrix.shape[:-2]
    rows_in = matrix.shape[-2]
    cols_in = matrix.shape[-1]
    row_blocks = pattern.shape[-2]
    col_blocks = pattern.shape[-1]
    tiled_grid = matrix.reshape(
        leading + (row_blocks, rows_in // row_blocks, col_blocks, cols_in // col_blocks)
    )
    keeper = pattern.astype(matrix.dtype)[..., :, None, :, None]
    return (tiled_grid * keeper).reshape(matrix.shape)


def convolve(activity, kernel):
    span_rows = activity.shape[2] - 2
    span_cols = activity.shape[3] - 2
    summed = jnp.zeros((kernel.shape[1], activity.shape[1], span_rows, span_cols), jnp.float32)
    for offset in range(9):
        row_off = offset // 3
        col_off = offset % 3
        window = activity[:, :, row_off : row_off + span_rows, col_off : col_off + span_cols]
        summed = summed + jnp.einsum("oc,cbhw->obhw", kernel[offset], window, precision=highest)
    return summed


def pad_both(activity):
    return jnp.pad(activity, ((0, 0), (0, 0), (1, 1), (1, 1)))


def pad_cols(activity):
    return jnp.pad(activity, ((0, 0), (0, 0), (0, 0), (1, 1)))


def kernels(first_in, middle, last_out):
    return (
        [first_in[:, :, None]]
        + [middle[member] for member in range(middle.shape[0])]
        + [last_out[:, None, :]]
    )


def denoise(volume, first_in, middle, last_out):
    kernel_list = kernels(first_in, middle, last_out)
    current = volume[None]
    for position, kernel in enumerate(kernel_list):
        current = convolve(pad_both(current), kernel)
        if position + 1 < len(kernel_list):
            current = jax.nn.relu(current)
    return volume - current[0]


def margin(activity, reach):
    return with_halo(activity, (("tile", 2),), reach)


def planar_pass(volume, kernel_list):
    layers_all = len(kernel_list)
    current = volume[None]
    for position, kernel in enumerate(kernel_list):
        current = convolve(pad_cols(margin(current, 1)), kernel)
        if position + 1 < layers_all:
            current = jax.nn.relu(current)
    return volume - current[0]


def plain_device(
    view_tile,
    block_mask,
    sinogram,
    bin_weight,
    model_state,
    planar_state,
    sagittal_state,
    planar_in,
    planar_mid,
    planar_out,
    sagittal_in,
    sagittal_mid,
    sagittal_out,
):
    slices_own = model_state.shape[1]
    voxels = model_state.shape[2]
    views_here = view_tile.shape[0]
    bins_all = view_tile.shape[2]
    masked = blocked(view_tile[:, 0], block_mask[:, 0])
    slices_all = slices_own * lax.axis_size("agent")
    rows_all = views_here * slices_all
    sino_rows = sinogram.reshape(rows_all, bins_all)
    weight_rows = bin_weight.reshape(rows_all, bins_all)
    own_anchor = model_state[0]
    guess_own = own_anchor
    guess_low = lax.all_gather(own_anchor.astype(jnp.bfloat16), "agent", axis=0, tiled=True)
    for iteration in range(GRAD_STEPS):
        partial_value = jnp.einsum(
            "sk,vbk->vsb", guess_low, masked, preferred_element_type=jnp.float32
        ).reshape(rows_all, bins_all)
        summed = lax.psum(partial_value, "tile")
        misfit = (weight_rows * (summed - sino_rows)).astype(jnp.bfloat16)
        misfit = misfit.reshape(views_here, slices_all, bins_all)
        grad_own = lax.psum_scatter(
            jnp.einsum("vsb,vbk->sk", misfit, masked, preferred_element_type=jnp.float32).astype(
                jnp.bfloat16
            ),
            "agent",
            scatter_dimension=0,
            tiled=True,
        ).astype(jnp.float32)
        guess_own = guess_own - step_size * (grad_own + prox_weight * (guess_own - own_anchor))
        if iteration + 1 < GRAD_STEPS:
            guess_low = lax.all_gather(guess_own.astype(jnp.bfloat16), "agent", axis=0, tiled=True)
    model_image = guess_own[None]
    plane_volume = planar_state[0].reshape(slices_own, PX, voxels // PX)
    plane_clean = planar_pass(plane_volume, kernels(planar_in, planar_mid, planar_out))
    planar_image = plane_clean.reshape(1, slices_own, voxels)
    side_volume = sagittal_state[0].reshape(slices_own, PX, voxels // PX)
    regrouped = lax.all_to_all(side_volume, "agent", split_axis=1, concat_axis=0, tiled=True)
    side_clean = denoise(
        regrouped.transpose(1, 0, 2), sagittal_in, sagittal_mid, sagittal_out
    ).transpose(1, 0, 2)
    returned = lax.all_to_all(side_clean, "agent", split_axis=0, concat_axis=1, tiled=True)
    sagittal_image = returned.reshape(1, slices_own, voxels)
    reflect_model = 2.0 * model_image - model_state
    reflect_plane = 2.0 * planar_image - planar_state
    reflect_side = 2.0 * sagittal_image - sagittal_state
    consensus = (
        share_model * reflect_model + share_plane * reflect_plane + share_side * reflect_side
    )
    model_next = (1.0 - relax_rate) * model_state + relax_rate * (2.0 * consensus - reflect_model)
    planar_next = (1.0 - relax_rate) * planar_state + relax_rate * (2.0 * consensus - reflect_plane)
    sagittal_next = (1.0 - relax_rate) * sagittal_state + relax_rate * (
        2.0 * consensus - reflect_side
    )
    return (model_next, planar_next, sagittal_next)


LANES = 128
FRAME = 16
HIGH_ROWS = 24
MESH = pl.DeviceIdType.MESH


def split_low(x):
    high = x.astype(jnp.bfloat16)
    low = (x - high.astype(jnp.float32)).astype(jnp.bfloat16)
    return high, low


def dot(a, b):
    return jnp.dot(a, b, preferred_element_type=jnp.float32)


def exact_dot(a, b):
    return jnp.dot(a, b, precision=highest, preferred_element_type=jnp.float32)


def iota(shape, dim):
    return lax.broadcasted_iota(jnp.int32, shape, dim)


def pack(x):
    half = x.shape[1] // 2
    return jnp.concatenate([x[:, :half], x[:, half:]], axis=0).astype(jnp.bfloat16)


def unpack(x):
    x = x.astype(jnp.float32)
    rows = x.shape[0] // 2
    return jnp.concatenate([x[:rows], x[rows:]], axis=1)


def column_shifts(h):
    lane = iota((h.shape[0], LANES), 1)
    befores, afters = [], []
    for start in range(0, h.shape[1], LANES):
        part = h[:, start : start + LANES]
        befores.append(jnp.where(lane == 0, 0.0, pltpu.roll(part, 1, axis=1)))
        afters.append(jnp.where(lane == LANES - 1, 0.0, pltpu.roll(part, LANES - 1, axis=1)))
    return jnp.concatenate(
        [jnp.concatenate(befores, axis=1), h, jnp.concatenate(afters, axis=1)], axis=0
    )


def build_weights(d, in_ref, mid_ref, out_ref, w_first, w_mid, w_last):
    layers, taps, hidden, _ = mid_ref.shape
    wide = FRAME * hidden
    spread = (iota((hidden, wide), 1) % hidden == iota((hidden, wide), 0)).astype(jnp.float32)
    gather = (iota((wide, hidden), 0) % hidden == iota((wide, hidden), 1)).astype(jnp.float32)
    columns = lax.dot_general(
        gather, in_ref[...], (((1,), (1,)), ((), ())), precision=highest,
        preferred_element_type=jnp.float32,
    )
    high, low = split_low(columns)
    high, low = high.astype(jnp.float32), low.astype(jnp.float32)
    depth = w_first.shape[2]
    offset = iota((wide, depth), 1) - iota((wide, depth), 0) // hidden
    first = jnp.zeros((wide, depth), jnp.float32)
    for turn, source in enumerate((high, high, low)):
        for tap in range(taps):
            a, e = tap // 3, tap % 3
            place = 3 * HIGH_ROWS * turn + HIGH_ROWS * e + a
            first = jnp.where(offset == place, source[:, tap : tap + 1], first)
    w_first[d] = first.astype(jnp.bfloat16)
    band = iota((wide, wide), 1) // hidden - iota((wide, wide), 0) // hidden
    for layer in range(layers):
        for e in range(3):
            value = jnp.zeros((wide, wide), jnp.float32)
            for a in range(3):
                tile = exact_dot(mid_ref[layer, 3 * a + e], spread)
                value = jnp.where(band == a - 1, jnp.concatenate([tile] * FRAME, axis=0), value)
            high, low = split_low(value)
            w_mid[d * layers + layer, 0, :, e * wide : (e + 1) * wide] = high
            w_mid[d * layers + layer, 1, :, e * wide : (e + 1) * wide] = low
    rows = exact_dot(out_ref[...], spread)
    margin_rows = layers
    shift = iota((PX, wide), 1) // hidden - iota((PX, wide), 0)
    for e in range(3):
        value = jnp.zeros((PX, wide), jnp.float32)
        for a in range(3):
            tap = 3 * a + e
            row = jnp.broadcast_to(rows[tap : tap + 1], (PX, wide))
            value = jnp.where(shift == margin_rows + a, row, value)
        high, low = split_low(value)
        both = jnp.concatenate([high.astype(jnp.float32), low.astype(jnp.float32)], axis=0)
        w_last[d, :, e * wide : (e + 1) * wide] = both.astype(jnp.bfloat16)


def denoise_unit(d, at, width, layers, hidden, place, count, field, w_first, w_mid, w_last, clean):
    lanes = slice(at, at + width)
    wide = FRAME * hidden
    frame_row = iota((wide, width), 0) // hidden
    above = (layers + 1) - place * PX
    below = (layers + 1) + (count - place) * PX
    inside = (frame_row >= above) & (frame_row < below)

    def active(x):
        return jnp.where(inside, jnp.maximum(x, 0.0), 0.0)

    shifted = column_shifts(field[d, :, lanes])
    high = shifted.astype(jnp.bfloat16).astype(jnp.float32)
    spare = w_first.shape[2] - 3 * shifted.shape[0]
    stacked = jnp.concatenate(
        [high, shifted - high, high, jnp.zeros((spare, width), jnp.float32)], axis=0
    ).astype(jnp.bfloat16)
    h = active(dot(w_first[d], stacked))

    for layer in range(layers):
        high, low = split_low(column_shifts(h))
        rows = slice((layer + 1) * hidden, (FRAME - 1 - layer) * hidden)
        w_high = w_mid[d * layers + layer, 0, rows]
        w_low = w_mid[d * layers + layer, 1, rows]
        h = dot(w_high, high) + dot(w_high, low) + dot(w_low, high)
        edge = jnp.zeros(((layer + 1) * hidden, width), jnp.float32)
        h = jnp.concatenate([edge, jnp.where(inside[rows], jnp.maximum(h, 0.0), 0.0), edge], axis=0)

    high, low = split_low(column_shifts(h))
    first = dot(w_last[d], high)
    second = dot(w_last[d], low)
    change = first[:PX] + first[PX : 2 * PX] + second[:PX]
    own = field[d, layers + 2 : layers + 2 + PX, lanes]
    clean[d, :, lanes] = own - change


def kernel(
    tiles, agents,
    view_hbm, mask_ref, sino_hbm, weight_hbm, model_ref, planar_ref, sagittal_ref,
    pin_ref, pmid_ref, pout_ref, sin_ref, smid_ref, sout_ref,
    model_out, planar_out, sagittal_out,
    masked, sino, weight, guess_all, part_send, part_recv, mis_all, grad_send, grad_recv,
    own_plane, halo, field, w_first, w_mid, w_last, clean,
    local_sem, send_agent, recv_agent, send_tile, recv_tile, send_halo, recv_halo,
):
    tile, agent = lax.axis_index("tile"), lax.axis_index("agent")
    views, bins = masked.shape[0], masked.shape[1]
    own_slices, voxels = model_ref.shape[1], model_ref.shape[2]
    layers, _, hidden, _ = pmid_ref.shape
    cells = voxels // PX
    slices_all = own_slices * agents

    load_view = pltpu.make_async_copy(view_hbm.at[:, 0], masked, local_sem.at[0])
    load_sino = pltpu.make_async_copy(sino_hbm.at[tile], sino, local_sem.at[1])
    load_weight = pltpu.make_async_copy(weight_hbm.at[tile], weight, local_sem.at[2])
    load_view.start()
    load_sino.start()
    load_weight.start()

    barrier = pltpu.get_barrier_semaphore()
    for k in range(1, agents):
        pl.semaphore_signal(
            barrier, inc=1, device_id=(tile, lax.rem(agent + k, agents)), device_id_type=MESH
        )
    for k in range(1, tiles):
        pl.semaphore_signal(
            barrier, inc=1, device_id=(lax.rem(tile + k, tiles), agent), device_id_type=MESH
        )
    anchor = model_ref[0]
    guess_all[0, agent] = pack(anchor)
    for row in range(PX):
        for piece in range(own_slices):
            own_plane[row : row + 1, piece * cells : (piece + 1) * cells] = planar_ref[
                0, piece : piece + 1, row * cells : (row + 1) * cells
            ]
    pl.semaphore_wait(barrier, agents + tiles - 2)

    sent = []

    def to_agent(src, dst, step, phase, k):
        copy = pltpu.make_async_remote_copy(
            src_ref=src, dst_ref=dst, send_sem=send_agent.at[step, phase, k],
            recv_sem=recv_agent.at[step, phase, k],
            device_id=(tile, lax.rem(agent + k, agents)), device_id_type=MESH,
        )
        copy.start()
        sent.append(copy)
        return copy

    def to_tile(src, dst, step, phase, k):
        copy = pltpu.make_async_remote_copy(
            src_ref=src, dst_ref=dst, send_sem=send_tile.at[step, phase, k],
            recv_sem=recv_tile.at[step, phase, k],
            device_id=(lax.rem(tile + k, tiles), agent), device_id_type=MESH,
        )
        copy.start()
        sent.append(copy)
        return copy

    def share_guess(step):
        return [
            to_agent(guess_all.at[step, agent], guess_all.at[step, agent], step, 0, k)
            for k in range(1, agents)
        ]

    waiting = share_guess(0)
    halos = []
    sides = (
        (own_plane, (lax.rem(tile + 1, tiles), agent)),
        (own_plane, (lax.rem(tile + tiles - 1, tiles), agent)),
        (sagittal_ref.at[0], (tile, lax.rem(agent + 1, agents))),
        (sagittal_ref.at[0], (tile, lax.rem(agent + agents - 1, agents))),
    )
    for k, (source, target) in enumerate(sides):
        copy = pltpu.make_async_remote_copy(
            src_ref=source, dst_ref=halo.at[k], send_sem=send_halo.at[k],
            recv_sem=recv_halo.at[k], device_id=target, device_id_type=MESH,
        )
        copy.start()
        halos.append(copy)
        sent.append(copy)

    build_weights(0, pin_ref, pmid_ref, pout_ref, w_first, w_mid, w_last)
    build_weights(1, sin_ref, smid_ref, sout_ref, w_first, w_mid, w_last)

    load_view.wait()
    row_blocks, col_blocks = mask_ref.shape[2], mask_ref.shape[3]
    block_rows, block_cols = bins // row_blocks, voxels // col_blocks
    widen = (
        iota((col_blocks, voxels), 1) // block_cols == iota((col_blocks, voxels), 0)
    ).astype(jnp.float32)
    for view in range(views):
        keep = exact_dot(mask_ref[view, 0].astype(jnp.float32), widen)
        for block in range(row_blocks):
            at = slice(block * block_rows, (block + 1) * block_rows)
            row = jnp.broadcast_to(keep[block : block + 1], (block_rows, voxels))
            masked[view, at] = masked[view, at] * row.astype(jnp.bfloat16)

    width = 4 * cells
    work = [(d, at) for d in range(2) for at in range(0, PX * cells, width)]
    places = ((tile, tiles), (agent, agents))

    def some_work():
        if work:
            d, at = work.pop(0)
            denoise_unit(
                d, at, width, layers, hidden, places[d][0], places[d][1],
                field, w_first, w_mid, w_last, clean,
            )

    def fill_fields():
        reach = layers + 2
        for copy in halos:
            copy.wait_recv()
        for d, own in ((0, own_plane[...]), (1, sagittal_ref[0])):
            place, count = places[d]
            low = halo[2 * d, PX - reach : PX]
            high = halo[2 * d + 1, 0:reach]
            field[d, 0:reach] = jnp.where(place > 0, low, jnp.zeros_like(low))
            field[d, reach : reach + PX] = own
            field[d, reach + PX : 2 * reach + PX] = jnp.where(
                place < count - 1, high, jnp.zeros_like(high)
            )
            rest = HIGH_ROWS - 2 * reach - PX
            field[d, 2 * reach + PX : HIGH_ROWS] = jnp.zeros((rest, PX * cells), jnp.float32)

    guess = anchor
    chunk = sino.shape[0]
    per_view = slices_all // chunk
    for step in range(GRAD_STEPS):
        for copy in waiting:
            copy.wait_recv()
        guess_low = jnp.concatenate(
            [unpack(guess_all[step, a]) for a in range(agents)], axis=0
        ).astype(jnp.bfloat16)
        for view in range(views):
            partial = lax.dot_general(
                guess_low, masked[view], (((1,), (1,)), ((), ())),
                preferred_element_type=jnp.float32,
            ).astype(jnp.bfloat16)
            for piece in range(per_view):
                part_send[step, view * per_view + piece] = partial[
                    piece * chunk : (piece + 1) * chunk
                ]
        waiting = [
            to_tile(
                part_send.at[step, lax.rem(tile + k, tiles)], part_recv.at[step, k], step, 0, k
            )
            for k in range(1, tiles)
        ]
        if step == 0:
            fill_fields()
            load_sino.wait()
            load_weight.wait()
        some_work()
        total = part_send[step, tile].astype(jnp.float32)
        for k, copy in enumerate(waiting):
            copy.wait_recv()
            total = total + part_recv[step, k + 1].astype(jnp.float32)
        mis_all[step, tile] = (weight[...] * (total - sino[...])).astype(jnp.bfloat16)
        waiting = [
            to_tile(mis_all.at[step, tile], mis_all.at[step, tile], step, 1, k)
            for k in range(1, tiles)
        ]
        some_work()
        for copy in waiting:
            copy.wait_recv()
        gradient = jnp.zeros((slices_all, voxels), jnp.float32)
        for view in range(views):
            misfit = jnp.concatenate(
                [mis_all[step, view * per_view + piece] for piece in range(per_view)], axis=0
            )
            gradient = gradient + dot(misfit, masked[view])
        for a in range(agents):
            grad_send[step, a] = pack(gradient[a * own_slices : (a + 1) * own_slices])
        waiting = [
            to_agent(
                grad_send.at[step, lax.rem(agent + k, agents)], grad_recv.at[step, k], step, 1, k
            )
            for k in range(1, agents)
        ]
        some_work()
        total = unpack(grad_send[step, agent])
        for k, copy in enumerate(waiting):
            copy.wait_recv()
            total = total + unpack(grad_recv[step, k + 1])
        guess = guess - step_size * (total + prox_weight * (guess - anchor))
        if step + 1 < GRAD_STEPS:
            guess_all[step + 1, agent] = pack(guess)
            waiting = share_guess(step + 1)
            some_work()
    while work:
        some_work()

    for row in range(PX):
        for piece in range(own_slices):
            planar_out[0, piece : piece + 1, row * cells : (row + 1) * cells] = clean[
                0, row : row + 1, piece * cells : (piece + 1) * cells
            ]
    planar_image = planar_out[0]
    sagittal_image = clean[1]
    planar_own, sagittal_own = planar_ref[0], sagittal_ref[0]
    reflect_model = 2.0 * guess - anchor
    reflect_plane = 2.0 * planar_image - planar_own
    reflect_side = 2.0 * sagittal_image - sagittal_own
    consensus = (
        share_model * reflect_model + share_plane * reflect_plane + share_side * reflect_side
    )
    keep_rate = 1.0 - relax_rate
    model_out[0] = keep_rate * anchor + relax_rate * (2.0 * consensus - reflect_model)
    planar_out[0] = keep_rate * planar_own + relax_rate * (2.0 * consensus - reflect_plane)
    sagittal_out[0] = keep_rate * sagittal_own + relax_rate * (2.0 * consensus - reflect_side)
    for copy in sent:
        copy.wait_send()


def per_device(*arguments):
    (view_tile, block_mask, sinogram, bin_weight, model_state, planar_state, sagittal_state,
     planar_in, planar_mid, planar_out, sagittal_in, sagittal_mid, sagittal_out) = arguments
    tiles, agents = lax.axis_size("tile"), lax.axis_size("agent")
    views, _, bins, voxels = view_tile.shape
    own_slices = model_state.shape[1]
    layers, taps, hidden, _ = planar_mid.shape
    rows_all = views * own_slices * agents
    chunk = rows_all // tiles
    fits = (
        chunk * tiles == rows_all
        and chunk % 16 == 0
        and (own_slices * agents) % chunk == 0
        and own_slices == PX
        and voxels == PX * LANES
        and PX + 2 * (layers + 1) <= FRAME
        and min(tiles, agents) > 1
    )
    if not fits:
        return plain_device(*arguments)
    bf16, f32 = jnp.bfloat16, jnp.float32
    vmem = pl.BlockSpec(memory_space=pltpu.VMEM)
    anywhere = pl.BlockSpec(memory_space=pl.ANY)
    wide = FRAME * hidden
    plane = (2 * own_slices, voxels // 2)
    depth = (9 * HIGH_ROWS + 15) // 16 * 16
    dma = pltpu.SemaphoreType.DMA
    return pl.pallas_call(
        functools.partial(kernel, tiles, agents),
        out_shape=[jax.ShapeDtypeStruct(model_state.shape, f32)] * 3,
        in_specs=[anywhere, vmem, anywhere, anywhere] + [vmem] * 9,
        out_specs=[vmem] * 3,
        scratch_shapes=[
            pltpu.VMEM((views, bins, voxels), bf16),
            pltpu.VMEM((chunk, bins), f32),
            pltpu.VMEM((chunk, bins), f32),
            pltpu.VMEM((GRAD_STEPS, agents) + plane, bf16),
            pltpu.VMEM((GRAD_STEPS, tiles, chunk, bins), bf16),
            pltpu.VMEM((GRAD_STEPS, tiles, chunk, bins), bf16),
            pltpu.VMEM((GRAD_STEPS, tiles, chunk, bins), bf16),
            pltpu.VMEM((GRAD_STEPS, agents) + plane, bf16),
            pltpu.VMEM((GRAD_STEPS, agents) + plane, bf16),
            pltpu.VMEM((PX, own_slices * (voxels // PX)), f32),
            pltpu.VMEM((4, PX, voxels), f32),
            pltpu.VMEM((2, HIGH_ROWS, voxels), f32),
            pltpu.VMEM((2, wide, depth), bf16),
            pltpu.VMEM((2 * layers, 2, wide, 3 * wide), bf16),
            pltpu.VMEM((2, 2 * PX, 3 * wide), bf16),
            pltpu.VMEM((2, PX, voxels), f32),
            dma((3,)),
            dma((GRAD_STEPS, 2, agents)),
            dma((GRAD_STEPS, 2, agents)),
            dma((GRAD_STEPS, 2, tiles)),
            dma((GRAD_STEPS, 2, tiles)),
            dma((4,)),
            dma((4,)),
        ],
        compiler_params=pltpu.CompilerParams(
            collective_id=0, has_side_effects=True, vmem_limit_bytes=48 * 1024 * 1024
        ),
    )(
        view_tile,
        block_mask,
        sinogram.reshape(tiles, chunk, bins),
        bin_weight.reshape(tiles, chunk, bins),
        model_state, planar_state, sagittal_state,
        planar_in, planar_mid, planar_out, sagittal_in, sagittal_mid, sagittal_out,
    )


def solution(mesh):
    return jax.shard_map(
        per_device,
        mesh=mesh,
        in_specs=(
            P("agent", "tile", None, None),
            P("agent", "tile", None, None),
            P("agent", None, None),
            P("agent", None, None),
            P("tile", "agent", None),
            P("tile", "agent", None),
            P("tile", "agent", None),
            P(),
            P(),
            P(),
            P(),
            P(),
            P(),
        ),
        out_specs=(P("tile", "agent", None), P("tile", "agent", None), P("tile", "agent", None)),
        check_vma=False,
    )
```
